256 devices in a mesh: lat: 8 (over y, core), wave: 16 (over x_lo, z), lev: 2 (over x_hi).
Axes of the slice: x: 4 (x_hi: 2, x_lo: 2; x = x_hi * 2 + x_lo), y: 4, z: 8, core: 2. Of those that a mesh axis runs over, the one named last changes fastest.
Arguments:
- fourier: bfloat16 [512, 2048, 256], P('wave', 'lat', 'lev'), may hold values from -6 to 6
- legendre: bfloat16 [512, 1024, 2, 1024], P('wave', 'lat', None, 'lev'), may hold values from -0.1875 to 0.1875
- wave_list: int32 [512], P('wave'), may hold values from 0 to 511, as said below
Outputs:
- spectra: bfloat16 [2, 512, 2, 512, 256], P(None, 'lat', None, 'wave', 'lev')
The draws below stay inside these ranges and needn't reach their ends.
Inputs may be any that keep to these rules, and one draw needn't show every extreme that they name: `wave_list`: A permutation of the slots; read in blocks of 32 entries, the entries k * 2 to (k + 1) * 2 - 1 of every block lie in k * 32 to (k + 1) * 32 - 1.
All inputs are finite; a program needn't handle non-finite values.
Results may differ from the reference program's by a relative error of at most 0.017.
Values may be sent and summed in bfloat16 or wider, within the bound.
No kernel may reach another device: no remote copies, remote signals or barrier semaphores. Data moves between devices by JAX's collectives and lax.ppermute only.
A program may use at most 128 MiB of HBM per device.

```python
import jax
import jax.numpy as jnp
from jax import lax

NN = 2048
LAT_DEV = 128
W_DEV = 32
COLS = 256
MW = 512
HLAT = 1024
NLAT = 2048
KSEND = 2
N_LAT = 8
N_WAVE = 16


def draw_wave_list(key, part):
    key = jax.random.fold_in(key, 11)
    key_rotation, key_flip = jax.random.split(key)
    source = jnp.arange(N_WAVE, dtype=jnp.int32)[:, None]
    local_rank = jnp.arange(W_DEV, dtype=jnp.int32)[None, :]
    cycle_pos = local_rank % (2 * N_WAVE)
    folded = jnp.where(cycle_pos < N_WAVE, cycle_pos, 2 * N_WAVE - 1 - cycle_pos)
    segment = local_rank // (2 * N_WAVE)
    flip_bits = jax.random.randint(key_flip, (N_WAVE, W_DEV // (2 * N_WAVE)), 0, 2)
    flip_at = jnp.take_along_axis(flip_bits, jnp.broadcast_to(segment, (N_WAVE, W_DEV)), axis=1)
    folded = jnp.where(flip_at == 1, N_WAVE - 1 - folded, folded)
    rotation = jax.random.randint(key_rotation, (N_WAVE, 1), 0, N_WAVE)
    target = (folded + rotation) % N_WAVE
    position = 2 * segment + (cycle_pos >= N_WAVE).astype(jnp.int32)
    values = source * W_DEV + local_rank
    sources_full = jnp.broadcast_to(source, (N_WAVE, W_DEV))
    positions_full = jnp.broadcast_to(position, (N_WAVE, W_DEV))
    listing = jnp.zeros((N_WAVE, N_WAVE, KSEND), jnp.int32)
    listing = listing.at[target, sources_full, positions_full].set(values)
    return listing.reshape(-1)


def with_spikes(values, own_key, source, target, shards_of, factor):
    def block_of(dim):
        return (jnp.arange(values.shape[dim]) // (values.shape[dim] // shards_of)).reshape((-1,) + (1,) * (values.ndim - 1 - dim))

    one_side = jax.random.permutation(own_key, shards_of)[block_of(target)]
    second = (block_of(target) + shards_of // 2) % shards_of
    return jnp.where((block_of(source) == one_side) | (block_of(source) == second), factor * values, values)


def block_scale(rng, dims, shards, low, high):
    gain, own = 1.0, jax.random.fold_in(rng, 6)
    for axis_at, shards_of in shards:
        draws = jnp.exp(jax.random.uniform(jax.random.fold_in(own, axis_at), (shards_of,), jnp.float32, low / len(shards), high / len(shards)))
        gain = gain * jnp.repeat(draws, dims[axis_at] // shards_of).reshape([-1 if axis == axis_at else 1 for axis in range(len(dims))])
    return gain


def centred(stream_key, dims, scale, reach, cuts=(), kind=jnp.bfloat16):
    entries = jax.random.normal(stream_key, dims, jnp.float32) * scale
    if len(cuts) > 0:
        entries = block_scale(stream_key, dims, cuts, -0.22, 0.18) * entries
    return jnp.clip(entries, min=-reach, max=reach).astype(kind)


def gaussian_with(key, shape, spread, limit, pieces, heavy, kind=jnp.bfloat16):
    array = spread * jax.random.normal(key, shape, jnp.float32)
    if pieces:
        array = array * block_scale(key, shape, pieces, -0.22, 0.18)
    return jnp.clip(with_spikes(array, jax.random.fold_in(key, 3), *heavy), -limit, limit).astype(kind)


def setup_inputs(seed: int = 0) -> dict:
    seeds = jax.random.split(jax.random.key(seed), 4)
    fourier = centred(seeds[0], (MW, NLAT, COLS), 1.0, 6.0, ((0, 16), (1, 8), (2, 2)))
    legendre = gaussian_with(seeds[1], (MW, HLAT, 2, NN // 2), (2 * HLAT) ** -0.5, 0.1875, ((0, 16), (1, 8), (3, 2)), (1, 3, 8, 2.0))
    wave_list = draw_wave_list(jax.random.fold_in(seeds[3], 71), 0)
    return {"fourier": fourier, "legendre": legendre, "wave_list": wave_list}


def reference(fourier, legendre, wave_list):
    ordered = jnp.take(fourier, wave_list, axis=0)
    band_rows = ordered.shape[1] // N_LAT
    half_rows = band_rows // 2
    banded = ordered.reshape(MW, N_LAT, band_rows, COLS)
    own_rows = banded[:, :, :half_rows].astype(jnp.float32)
    mirror_rows = banded[:, ::-1, half_rows:][:, :, ::-1].astype(jnp.float32)
    folded_sum = (own_rows + mirror_rows).astype(jnp.bfloat16)
    folded_diff = (own_rows - mirror_rows).astype(jnp.bfloat16)
    parity = wave_list % 2
    sources = []
    for degree_parity in range(2):
        pick = ((parity + degree_parity) % 2 == 0)[:, None, None, None]
        sources.append(jnp.where(pick, folded_sum, folded_diff))
    paired = jnp.stack(sources, axis=0)
    group_count = MW // W_DEV
    table_groups = legendre.reshape(group_count, W_DEV, N_LAT, LAT_DEV, 2, NN // 2)
    field_groups = paired.reshape(2, group_count, W_DEV, N_LAT, LAT_DEV, COLS).transpose(1, 0, 2, 3, 4, 5)

    def one_group(operands):
        table_group, fields_group = operands

        def add_band(running, band):
            band_table = lax.dynamic_index_in_dim(table_group, band, axis=1, keepdims=False).astype(jnp.float32)
            band_fields = lax.dynamic_index_in_dim(fields_group, band, axis=2, keepdims=False).astype(jnp.float32)
            partial_value = jnp.einsum("slpq,pslc->qpsc", band_table, band_fields)
            rounded = lax.optimization_barrier(partial_value.astype(jnp.bfloat16))
            return running + rounded.astype(jnp.float32), None

        start = jnp.zeros((NN // 2, 2, W_DEV, COLS), jnp.float32)
        running, unused = lax.scan(add_band, start, jnp.arange(N_LAT, dtype=jnp.int32))
        return running

    totals = lax.map(one_group, (table_groups, field_groups))
    total = totals.transpose(1, 2, 0, 3, 4).reshape(NN // 2, 2, MW, COLS)
    stride = NN // MW
    q_index = jnp.arange(NN // 2, dtype=jnp.int32)
    degrees = 2 * q_index[:, None] + jnp.arange(2, dtype=jnp.int32)[None, :]
    lowest = wave_list * stride + (wave_list % 2) * (stride - 1)
    keep_mask = degrees[:, :, None] >= lowest[None, None, :]
    spectra = jnp.where(keep_mask[..., None], total, 0.0).astype(jnp.bfloat16)
    return spectra.reshape(2, NN // 4, 2, MW, COLS)
```

```python
import functools

import jax
import jax.numpy as jnp
from jax import lax
from jax.experimental import pallas as pl
from jax.experimental.pallas import tpu as pltpu
from jax.sharding import PartitionSpec as P

NN = 2048
HOPS = (2, 6, 3, 7, 4, 5, 1)


def after(first, *arrays):
    return lax.optimization_barrier((first, *arrays))[1:]


def narrow_kernel(place, table, *refs):
    outs, sems = refs[:8], refs[8]
    lat, lev = place[0], place[1]
    width = table.shape[3] // 4
    copies = []
    for hop in range(8):
        band = lat ^ hop
        skip = band // 2
        for n in range(5):
            first = n < 4 - skip
            slot = jnp.where(first, 2 * band, 15 - 2 * band) + 16 * lev
            tile = jnp.where(first, skip + n, n - 1)
            copies.append(
                pltpu.make_async_copy(
                    table.at[slot, :, :, pl.ds(pl.multiple_of(tile * width, width), width)],
                    outs[hop].at[:, :, n * width : (n + 1) * width],
                    sems.at[hop, n],
                )
            )
    for copy in copies:
        copy.start()
    for copy in copies:
        copy.wait()


def wide_kernel(place, table, crossed, *refs):
    outs, sems = refs[:8], refs[8]
    lat, lev = place[0], place[1]

    def copies(pick):
        return [
            pltpu.make_async_copy(pick(lat ^ hop), outs[hop], sems.at[hop]) for hop in range(8)
        ]

    @pl.when(lev == 0)
    def _():
        for copy in copies(lambda band: crossed.at[band]):
            copy.start()

    @pl.when(lev != 0)
    def _():
        for copy in copies(lambda band: table.at[2 * band + 1]):
            copy.start()

    for copy in copies(lambda band: crossed.at[0]):
        copy.wait()


def transform_kernel(place, *refs):
    wide, narrow, fields = refs[:8], refs[8:16], refs[16]
    out, table, source, sems = refs[17:]
    lat = place[0]
    rows = wide[0].shape[1]
    reach = wide[0].shape[2]
    width = reach // 4
    cols = fields.shape[3]
    copies = []
    for hop in range(8):
        span = pl.ds(hop * rows, rows)
        copies.append(
            pltpu.make_async_copy(wide[hop], table.at[:, span, 0:reach], sems.at[0, hop])
        )
        copies.append(
            pltpu.make_async_copy(
                narrow[hop], table.at[:, span, reach : reach + 5 * width], sems.at[1, hop]
            )
        )
    for copy in copies:
        copy.start()
    out[...] = jnp.zeros_like(out)
    at_row = lax.broadcasted_iota(jnp.int32, (rows, rows), 0)
    at_col = lax.broadcasted_iota(jnp.int32, (rows, rows), 1)
    flip = (at_row + at_col == rows - 1).astype(jnp.bfloat16)
    pairs = [(f, v) for f in range(3) for v in range(2)]
    for hop in range(8):
        band = lat ^ hop
        near = [fields[2 * band + v, f, 0:rows, :] for f, v in pairs]
        far = [fields[2 * (7 - band) + v, f, rows : 2 * rows, :] for f, v in pairs]
        mirrored = jnp.dot(flip, jnp.concatenate(far, 1), preferred_element_type=jnp.float32)
        for n, (f, v) in enumerate(pairs):
            one = near[n].astype(jnp.float32)
            other = mirrored[:, n * cols : (n + 1) * cols]
            odd = place[2 + f] == 1
            other = jnp.where(odd, -other, other)
            here = (slice(hop * rows, (hop + 1) * rows), slice(v * cols, (v + 1) * cols))
            source[f, 0, *here] = (one + other).astype(jnp.bfloat16)
            source[f, 1, *here] = (one - other).astype(jnp.bfloat16)
    for copy in copies:
        copy.wait()
    half = width // 2

    def product(p, f, first):
        return lax.dot_general(
            table[p, :, first : first + width],
            source[f, p],
            (((0,), (0,)), ((), ())),
            preferred_element_type=jnp.float32,
        ).astype(jnp.bfloat16)

    skip = lat // 2
    for p in range(2):
        for n in range(4):
            values = product(p, 0, n * width)
            for h in range(2):
                for v in range(2):
                    out[2 * (2 * n + h) + v, 0, p] = values[
                        h * half : (h + 1) * half, v * cols : (v + 1) * cols
                    ]
        for n in range(5):
            first = n < 4 - skip
            f = jnp.where(first, 1, 2)
            tile = jnp.where(first, skip + n, n - 1)
            values = product(p, f, reach + n * width)
            for h in range(2):
                for v in range(2):
                    out[2 * (2 * tile + h) + v, f, p] = values[
                        h * half : (h + 1) * half, v * cols : (v + 1) * cols
                    ]


def degree_mask(slot_ids, first_q, q_count, stride):
    q_index = first_q + jnp.arange(q_count, dtype=jnp.int32)
    degrees = 2 * q_index[:, None] + jnp.arange(2, dtype=jnp.int32)[None, :]
    lowest = slot_ids * stride + slot_ids % 2 * (stride - 1)
    return degrees[:, :, None] >= lowest[None, None, :]


def shards(fourier, legendre, wave_list):
    any_space = pl.BlockSpec(memory_space=pl.ANY)
    smem = pl.BlockSpec(memory_space=pltpu.SMEM)
    vmem = pl.BlockSpec(memory_space=pltpu.VMEM)
    lat, lev = lax.axis_index("lat"), lax.axis_index("lev")
    block_id = lax.axis_index("wave")
    slot_count, row_count, cols = fourier.shape
    bands, blocks = lax.axis_size("lat"), lax.axis_size("wave")
    rows, reach = legendre.shape[1], legendre.shape[3]
    width = reach // 4
    stride = NN // (slot_count * blocks)

    cross = jnp.transpose(legendre[0:16:2], (0, 2, 1, 3))
    crossed = lax.ppermute(cross, "lev", [(1, 0)])

    wanted = lax.all_to_all(wave_list.reshape(blocks, -1), "wave", 0, 0, tiled=True)
    outgoing = jnp.take(fourier, (wanted - block_id * slot_count).reshape(-1), axis=0)
    arrived = lax.all_to_all(outgoing, "wave", 0, 0, tiled=True)

    place = jnp.stack([lat, lev]).astype(jnp.int32)
    table = jnp.transpose(legendre, (0, 2, 1, 3))
    narrow_shape = jax.ShapeDtypeStruct((2, rows, 5 * width), jnp.bfloat16)
    narrow = pl.pallas_call(
        narrow_kernel,
        in_specs=[smem, any_space],
        out_specs=[any_space] * 8,
        out_shape=[narrow_shape] * 8,
        scratch_shapes=[pltpu.SemaphoreType.DMA((8, 5))],
    )(place, table)
    narrow = list(narrow)
    for hop in HOPS:
        narrow[hop] = lax.ppermute(narrow[hop], "lat", [(i, i ^ hop) for i in range(bands)])
    wide_shape = jax.ShapeDtypeStruct((2, rows, reach), jnp.bfloat16)
    wide = pl.pallas_call(
        wide_kernel,
        in_specs=[smem, any_space, any_space],
        out_specs=[any_space] * 8,
        out_shape=[wide_shape] * 8,
        scratch_shapes=[pltpu.SemaphoreType.DMA((8,))],
    )(place, table, crossed)
    wide = list(wide)
    for hop in HOPS:
        wide[hop] = lax.ppermute(wide[hop], "lat", [(i, i ^ hop) for i in range(bands)])

    order = []
    for m in range(bands):
        order += [2 * m, 2 * m, 15 - 2 * m, 2 * m + 1, 16 + 2 * m, 31 - 2 * m]
    handled = jnp.take(arrived, jnp.array(order, jnp.int32), axis=0)
    handled = handled.reshape(2 * bands, 3, row_count, cols)
    fields = lax.all_to_all(handled, ("lat", "lev"), 0, 0, tiled=True)

    mine = lax.dynamic_index_in_dim(
        jnp.array(order, jnp.int32).reshape(2 * bands, 3), 2 * lat + lev, 0, keepdims=False
    )
    parity = jnp.take(wave_list, mine) % 2
    coefficients = pl.pallas_call(
        transform_kernel,
        in_specs=[smem] + [any_space] * 16 + [vmem],
        out_specs=vmem,
        out_shape=jax.ShapeDtypeStruct((2 * bands, 3, 2, width // 2, cols), jnp.bfloat16),
        scratch_shapes=[
            pltpu.VMEM((2, bands * rows, reach + 5 * width), jnp.bfloat16),
            pltpu.VMEM((3, 2, bands * rows, 2 * cols), jnp.bfloat16),
            pltpu.SemaphoreType.DMA((2, 8)),
        ],
        compiler_params=pltpu.CompilerParams(vmem_limit_bytes=40 * 1024 * 1024),
    )(jnp.concatenate([place, parity]), *wide, *narrow, fields)

    owned = lax.all_to_all(coefficients, ("lat", "lev"), 0, 0, tiled=True)
    owned = owned.reshape(bands, 2, 3, 2, width // 2, cols)

    def woven(even, odd):
        return jnp.stack([even, odd], axis=1).reshape(2 * bands, *even.shape[1:])

    low = woven(owned[:, 0, 1], owned[::-1, 0, 2])
    high = jnp.concatenate(
        [woven(owned[:, 0, 0], owned[:, 1, 0]), woven(owned[:, 1, 1], owned[::-1, 1, 2])]
    )
    spectra = jnp.stack([jnp.concatenate([low, jnp.zeros_like(low)]), high])
    spectra = jnp.transpose(spectra, (0, 3, 2, 1, 4))
    piece = width // 2
    keep = jnp.stack(
        [degree_mask(wave_list, k * reach + lat * piece, piece, stride) for k in range(2)]
    )
    return jnp.where(keep[..., None], spectra, 0).astype(jnp.bfloat16)


def solution(mesh):
    placed = (P("wave", "lat", "lev"), P("wave", "lat", None, "lev"), P("wave"))
    return jax.shard_map(
        shards,
        mesh=mesh,
        in_specs=placed,
        out_specs=P(None, "lat", None, "wave", "lev"),
        check_vma=False,
    )
```

```python
import functools

import jax
import jax.numpy as jnp
from jax import lax
from jax.experimental import pallas as pl
from jax.experimental.pallas import tpu as pltpu
from jax.sharding import PartitionSpec as P

NN = 2048
FIRST = (2, 6, 4)
LAST = (3, 7, 5, 1)


def after(first, *arrays):
    return lax.optimization_barrier((first, *arrays))[1:]


def first_kernel(place, table, *outs):
    for out, hop in zip(outs, FIRST):
        band = place[0] ^ hop
        out[0] = table[band]
        out[1] = table[15 - band]


def rest_kernel(place, table, wide, slim, *outs):
    lat, lev = place[0], place[1]
    reach, cut, end = table.shape[3], wide.shape[3], slim.shape[3]

    def lone(out, band):
        @pl.when(lev == 0)
        def _():
            out[:, :, 0 : reach - cut] = jnp.zeros_like(out[:, :, 0 : reach - cut])

            @pl.when(band < 4)
            def _():
                out[:, :, reach - cut :] = wide[band]

            @pl.when(band >= 4)
            def _():
                out[:, :, reach - cut : reach - end] = jnp.zeros_like(slim[0])
                out[:, :, reach - end :] = slim[band - 4]

        @pl.when(lev != 0)
        def _():
            out[...] = table[16 + band]

    for out, hop in zip(outs[:3], FIRST):
        lone(out, lat ^ hop)
    for out, hop in zip(outs[3:], (0, *LAST)):
        band = lat ^ hop
        out[0] = table[band]
        out[1] = table[15 - band]
        lone(out.at[2], band)


def transform_kernel(place, *refs):
    first, lone, whole, arrived, out, source, table, fields, sems = refs[:3], refs[3:6], refs[6:11], *refs[11:]
    lat = place[0]
    rows, reach = table.shape[2] // 8, table.shape[3]
    width = reach // 4
    half = width // 2
    cols = fields.shape[3]
    fetch = [pltpu.make_async_copy(arrived, fields, sems.at[11])]
    spans = {hop: pl.ds(hop * rows, rows) for hop in range(8)}
    for n, hop in enumerate(FIRST):
        fetch.append(pltpu.make_async_copy(first[n], table.at[0:2, :, spans[hop]], sems.at[n]))
        fetch.append(pltpu.make_async_copy(lone[n], table.at[2, :, spans[hop]], sems.at[3 + n]))
    for n, hop in enumerate((0, *LAST)):
        fetch.append(pltpu.make_async_copy(whole[n], table.at[:, :, spans[hop]], sems.at[6 + n]))
    for copy in fetch:
        copy.start()
    at_row = lax.broadcasted_iota(jnp.int32, (rows, rows), 0)
    at_col = lax.broadcasted_iota(jnp.int32, (rows, rows), 1)
    flip = (at_row + at_col == rows - 1).astype(jnp.bfloat16)
    fetch[0].wait()
    pairs = [(f, v) for f in range(3) for v in range(2)]
    for hop in range(8):
        band = lat ^ hop
        near = [fields[2 * band + v, f, 0:rows, :] for f, v in pairs]
        far = [fields[2 * (7 - band) + v, f, rows : 2 * rows, :] for f, v in pairs]
        mirrored = jnp.dot(flip, jnp.concatenate(far, 1), preferred_element_type=jnp.float32)
        for n, (f, v) in enumerate(pairs):
            one = near[n].astype(jnp.float32)
            other = mirrored[:, n * cols : (n + 1) * cols]
            odd = place[2 + f] == 1
            other = jnp.where(odd, -other, other)
            here = (slice(hop * rows, (hop + 1) * rows), slice(v * cols, (v + 1) * cols))
            source[f, 0, *here] = (one + other).astype(jnp.bfloat16)
            source[f, 1, *here] = (one - other).astype(jnp.bfloat16)
    for copy in fetch[1:]:
        copy.wait()
    for f in range(3):
        for p in range(2):
            for n in range(4):
                values = lax.dot_general(
                    table[f, p, :, n * width : (n + 1) * width],
                    source[f, p],
                    (((0,), (0,)), ((), ())),
                    preferred_element_type=jnp.float32,
                ).astype(jnp.bfloat16)
                for h in range(2):
                    for v in range(2):
                        out[2 * (2 * n + h) + v, f, p] = values[
                            h * half : (h + 1) * half, v * cols : (v + 1) * cols
                        ]


def pick_kernel(order, arrived, out):
    for n, slot in enumerate(order):
        out[n // 3, n % 3] = arrived[slot]


def spread_kernel(place, lowest, owned, out):
    piece, slots, cols = out.shape[1], out.shape[3], out.shape[4]
    bands = slots // 4
    up = range(bands)
    down = range(bands - 1, -1, -1)
    whole = [
        [(2 * m, 0) for m in up] + [(2 * m, 1) for m in down],
        [(2 * m + 1, 0) for m in up]
        + [(2 * m + 1, 1) for m in down]
        + [(2 * m + 1, 2) for m in up]
        + [(2 * m, 2) for m in up],
    ]
    for k in range(2):
        count = len(whole[k])
        q = lax.broadcasted_iota(jnp.int32, (piece, count, cols), 0) + (8 * k + place[0]) * piece
        for p in range(2):
            held = jnp.stack([owned[n, e, p].astype(jnp.float32) for n, e in whole[k]])
            held = jnp.transpose(held, (1, 0, 2))
            held = jnp.where(2 * q + p >= lowest[0:count][None], held, 0.0)
            out[k, :, p, 0:count] = held.astype(jnp.bfloat16)
            if count < slots:
                out[k, :, p, count:] = jnp.zeros((piece, slots - count, cols), jnp.bfloat16)


def shards(fourier, legendre, wave_list):
    roomy = pltpu.CompilerParams(vmem_limit_bytes=8 * 1024 * 1024)
    any_space = pl.BlockSpec(memory_space=pl.ANY)
    smem = pl.BlockSpec(memory_space=pltpu.SMEM)
    vmem = pl.BlockSpec(memory_space=pltpu.VMEM)
    lat, lev = lax.axis_index("lat"), lax.axis_index("lev")
    block_id = lax.axis_index("wave")
    slot_count, row_count, cols = fourier.shape
    bands, blocks = lax.axis_size("lat"), lax.axis_size("wave")
    rows, reach = legendre.shape[1], legendre.shape[3]
    width = reach // 4
    stride = NN // (slot_count * blocks)

    def hopped(array, hop):
        return lax.ppermute(array, "lat", [(i, i ^ hop) for i in range(bands)])

    def shape_of(*dims):
        return jax.ShapeDtypeStruct(dims, jnp.bfloat16)

    wide = legendre[24:28, :, :, reach // 2 :]
    slim = legendre[28:32, :, :, reach - width :]
    wide, slim, listing, legendre = lax.optimization_barrier((wide, slim, wave_list, legendre))
    wide = lax.ppermute(wide, "lev", [(1, 0)])
    slim = lax.ppermute(slim, "lev", [(1, 0)])

    wanted = lax.all_to_all(listing.reshape(blocks, -1), "wave", 0, 0, tiled=True)
    local = (wanted - block_id * slot_count).reshape(-1)
    outgoing = jnp.take(fourier, local, axis=0, mode="clip")

    place = jnp.stack([lat, lev]).astype(jnp.int32)
    first = pl.pallas_call(
        first_kernel,
        in_specs=[smem, vmem],
        out_specs=[vmem] * 3,
        out_shape=[shape_of(2, rows, 2, reach)] * 3,
        compiler_params=roomy,
    )(place, legendre)
    outgoing, wide, slim, *first = lax.optimization_barrier((outgoing, wide, slim, *first))
    arrived = lax.all_to_all(outgoing, "wave", 0, 0, tiled=True)
    first = [hopped(array, hop) for array, hop in zip(first, FIRST)]
    rest = pl.pallas_call(
        rest_kernel,
        in_specs=[smem] + [vmem] * 3,
        out_specs=[vmem] * 8,
        out_shape=[shape_of(rows, 2, reach)] * 3 + [shape_of(3, rows, 2, reach)] * 5,
        compiler_params=roomy,
    )(place, legendre, wide, slim)
    lone, (mine, *whole) = rest[:3], rest[3:]
    whole = [mine] + [hopped(array, hop) for array, hop in zip(whole, LAST)]
    lone = [hopped(array, hop) for array, hop in zip(lone, FIRST)]
    arrived, first, whole[:3] = lax.optimization_barrier((arrived, first, whole[:3]))

    order = []
    for m in range(bands):
        order += [m, 15 - m, 24 + m, m, 15 - m, 16 + m]
    handled = pl.pallas_call(
        functools.partial(pick_kernel, order),
        in_specs=[vmem],
        out_specs=vmem,
        out_shape=jax.ShapeDtypeStruct((2 * bands, 3, row_count, cols), jnp.bfloat16),
        compiler_params=roomy,
    )(arrived)
    handled, first, lone, whole = lax.optimization_barrier((handled, first, lone, whole))
    first = [jnp.transpose(array, (0, 2, 1, 3)) for array in first]
    lone = [jnp.transpose(array, (1, 0, 2)) for array in lone]
    whole = [jnp.transpose(array, (0, 2, 1, 3)) for array in whole]
    fields = lax.all_to_all(handled, ("lat", "lev"), 0, 0, tiled=True)

    handling = lax.dynamic_index_in_dim(
        jnp.array(order, jnp.int32).reshape(2 * bands, 3), 2 * lat + lev, 0, keepdims=False
    )
    parity = jnp.take(wave_list, handling, mode="clip") % 2
    coefficients = pl.pallas_call(
        transform_kernel,
        in_specs=[smem] + [any_space] * 12,
        out_specs=vmem,
        out_shape=jax.ShapeDtypeStruct((2 * bands, 3, 2, width // 2, cols), jnp.bfloat16),
        scratch_shapes=[
            pltpu.VMEM((3, 2, bands * rows, 2 * cols), jnp.bfloat16),
            pltpu.VMEM((3, 2, bands * rows, reach), jnp.bfloat16),
            pltpu.VMEM((2 * bands, 3, row_count, cols), jnp.bfloat16),
            pltpu.SemaphoreType.DMA((12,)),
        ],
        compiler_params=pltpu.CompilerParams(vmem_limit_bytes=60 * 1024 * 1024),
    )(jnp.concatenate([place, parity]), *first, *lone, *whole, fields)

    owned = lax.all_to_all(coefficients, ("lat", "lev"), 0, 0, tiled=True)
    piece = width // 2
    lowest = wave_list * stride + wave_list % 2 * (stride - 1)
    lowest = jnp.broadcast_to(lowest[:, None], (slot_count, cols))
    return pl.pallas_call(
        spread_kernel,
        in_specs=[smem, vmem, vmem],
        out_specs=vmem,
        out_shape=jax.ShapeDtypeStruct((2, piece, 2, slot_count, cols), jnp.bfloat16),
        compiler_params=roomy,
    )(place, lowest, owned)


def solution(mesh):
    placed = (P("wave", "lat", "lev"), P("wave", "lat", None, "lev"), P("wave"))
    return jax.shard_map(
        shards,
        mesh=mesh,
        in_specs=placed,
        out_specs=P(None, "lat", None, "wave", "lev"),
        check_vma=False,
    )
```

```python
import functools

import jax
import jax.numpy as jnp
from jax import lax
from jax.experimental import pallas as pl
from jax.experimental.pallas import tpu as pltpu
from jax.sharding import PartitionSpec as P

NN = 2048
FIRST = (2, 6, 4)
LAST = (3, 7, 5, 1)


def band_to(lat, hop):
    if hop in (2, 3):
        return lat ^ (hop + 4 * (lat % 2))
    if hop in (6, 7):
        return lat ^ (hop - 4 * (lat % 2))
    return lat ^ hop


def band_from(lat, hop):
    if hop == 3:
        return lat ^ (7 - 4 * (lat % 2))
    if hop == 7:
        return lat ^ (3 + 4 * (lat % 2))
    return band_to(lat, hop)


def after(first, *arrays):
    return lax.optimization_barrier((first, *arrays))[1:]


def first_kernel(place, table, *refs):
    outs, cross, sems = refs[:3], *refs[3:]
    reach, cut = table.shape[3], cross.shape[3]
    copies = [
        pltpu.make_async_copy(table.at[24:28, :, :, reach - cut : reach], cross.at[0:4], sems.at[6])
    ]
    for n in range(4):
        lanes = slice(n % 2 * cut // 2, (n % 2 + 1) * cut // 2)
        copies.append(
            pltpu.make_async_copy(
                table.at[28 + n, :, :, reach - cut // 2 : reach],
                cross.at[4 + n // 2, :, :, lanes],
                sems.at[7 + n],
            )
        )
    for n, hop in enumerate(FIRST):
        band = band_to(place[0], hop)
        copies += [
            pltpu.make_async_copy(table.at[band], outs[n].at[0], sems.at[2 * n]),
            pltpu.make_async_copy(table.at[15 - band], outs[n].at[1], sems.at[2 * n + 1]),
        ]
    for copy in copies:
        copy.start()
    for copy in copies:
        copy.wait()


def rest_kernel(place, table, cross, *refs):
    outs, sems = refs[:8], refs[8]
    lat, lev = place[0], place[1]
    reach, cut = table.shape[3], cross.shape[3]
    end = cut // 2
    copies, lone = [], []
    for n, hop in enumerate((*FIRST, 0, *LAST)):
        band, out = band_to(lat, hop), outs[n]
        if n >= 3:
            copies += [
                pltpu.make_async_copy(table.at[band], out.at[0], sems.at[n, 0]),
                pltpu.make_async_copy(table.at[15 - band], out.at[1], sems.at[n, 1]),
            ]
            out = out.at[2]
        lone.append((band, out, pltpu.make_async_copy(table.at[16 + band], out, sems.at[n, 2])))
    for copy in copies:
        copy.start()

    @pl.when(lev == 0)
    def _():
        for band, out, _ in lone:
            out[:, :, 0 : reach - cut] = jnp.zeros_like(out[:, :, 0 : reach - cut])

            @pl.when(band < 4)
            def _():
                out[:, :, reach - cut :] = cross[band]

            @pl.when(band >= 4)
            def _():
                lanes = pl.ds(pl.multiple_of(band % 2 * end, end), end)
                out[:, :, reach - cut : reach - end] = jnp.zeros_like(out[:, :, 0:end])
                out[:, :, reach - end :] = cross[2 + band // 2, :, :, lanes]

    @pl.when(lev != 0)
    def _():
        for _, _, copy in lone:
            copy.start()
        for _, _, copy in lone:
            copy.wait()

    for copy in copies:
        copy.wait()


def pack_kernel(*refs):
    first, lone, whole, out = refs[:3], refs[3:6], refs[6:11], refs[11]
    rows = lone[0].shape[0]
    for n, hop in enumerate((*FIRST, 0, *LAST)):
        for f in range(3):
            if n >= 3:
                values = whole[n - 3][f]
            else:
                values = first[n][f] if f < 2 else lone[n][...]
            out[f, :, hop * rows : (hop + 1) * rows, :] = jnp.swapaxes(values, 0, 1)


def transform_kernel(place, *refs):
    packed, arrived, out, source, table, fields, sems = refs
    lat = place[0]
    rows, reach = table.shape[2] // 8, table.shape[3]
    width = reach // 4
    half = width // 2
    cols = arrived.shape[3]
    fetch = pltpu.make_async_copy(arrived, fields, sems.at[0])
    fetch.start()
    load = pltpu.make_async_copy(packed, table, sems.at[1])
    load.start()
    at_row = lax.broadcasted_iota(jnp.int32, (rows, rows), 0)
    at_col = lax.broadcasted_iota(jnp.int32, (rows, rows), 1)
    flip = (at_row + at_col == rows - 1).astype(jnp.bfloat16)
    fetch.wait()
    pairs = [(f, v) for f in range(3) for v in range(2)]
    for hop in range(8):
        band = band_from(lat, hop)
        near = [fields[2 * band + v, f, 0:rows, :] for f, v in pairs]
        far = [fields[2 * (7 - band) + v, f, rows : 2 * rows, :] for f, v in pairs]
        mirrored = jnp.dot(flip, jnp.concatenate(far, 1), preferred_element_type=jnp.float32)
        for n, (f, v) in enumerate(pairs):
            one = near[n].astype(jnp.float32)
            other = mirrored[:, n * cols : (n + 1) * cols]
            odd = place[2 + f] == 1
            other = jnp.where(odd, -other, other)
            here = (slice(hop * rows, (hop + 1) * rows), slice(v * cols, (v + 1) * cols))
            source[f, 0, *here] = (one + other).astype(jnp.bfloat16)
            source[f, 1, *here] = (one - other).astype(jnp.bfloat16)
    load.wait()
    for f in range(3):
        for p in range(2):
            for n in range(4):
                values = lax.dot_general(
                    table[f, p, :, n * width : (n + 1) * width],
                    source[f, p],
                    (((0,), (0,)), ((), ())),
                    preferred_element_type=jnp.float32,
                ).astype(jnp.bfloat16)
                for h in range(2):
                    for v in range(2):
                        out[2 * (2 * n + h) + v, f, p] = values[
                            h * half : (h + 1) * half, v * cols : (v + 1) * cols
                        ]


def pick_kernel(order, arrived, out):
    for n, slot in enumerate(order):
        out[n // 3, n % 3] = arrived[slot]


def spread_kernel(place, lowest, owned, out):
    piece, slots, cols = out.shape[1], out.shape[3], out.shape[4]
    bands = slots // 4
    up = range(bands)
    down = range(bands - 1, -1, -1)
    whole = [
        [(2 * m, 0) for m in up] + [(2 * m, 1) for m in down],
        [(2 * m + 1, 0) for m in up]
        + [(2 * m + 1, 1) for m in down]
        + [(2 * m + 1, 2) for m in up]
        + [(2 * m, 2) for m in up],
    ]
    for k in range(2):
        count = len(whole[k])
        q = lax.broadcasted_iota(jnp.int32, (piece, count, cols), 0) + (8 * k + place[0]) * piece
        for p in range(2):
            held = jnp.stack([owned[n, e, p].astype(jnp.float32) for n, e in whole[k]])
            held = jnp.transpose(held, (1, 0, 2))
            held = jnp.where(2 * q + p >= lowest[0:count][None], held, 0.0)
            out[k, :, p, 0:count] = held.astype(jnp.bfloat16)
            if count < slots:
                out[k, :, p, count:] = jnp.zeros((piece, slots - count, cols), jnp.bfloat16)


def shards(fourier, legendre, wave_list):
    roomy = pltpu.CompilerParams(vmem_limit_bytes=8 * 1024 * 1024)
    any_space = pl.BlockSpec(memory_space=pl.ANY)
    smem = pl.BlockSpec(memory_space=pltpu.SMEM)
    vmem = pl.BlockSpec(memory_space=pltpu.VMEM)
    lat, lev = lax.axis_index("lat"), lax.axis_index("lev")
    block_id = lax.axis_index("wave")
    slot_count, row_count, cols = fourier.shape
    bands, blocks = lax.axis_size("lat"), lax.axis_size("wave")
    rows, reach = legendre.shape[1], legendre.shape[3]
    width = reach // 4
    stride = NN // (slot_count * blocks)

    def hopped(array, hop):
        return lax.ppermute(array, "lat", [(i, band_to(i, hop)) for i in range(bands)])

    def shape_of(*dims):
        return jax.ShapeDtypeStruct(dims, jnp.bfloat16)

    place = jnp.stack([lat, lev]).astype(jnp.int32)
    full = pltpu.CompilerParams(vmem_limit_bytes=56 * 1024 * 1024)
    *first, cross = pl.pallas_call(
        first_kernel,
        in_specs=[smem, any_space],
        out_specs=[vmem] * 4,
        out_shape=[shape_of(2, rows, 2, reach)] * 3 + [shape_of(6, rows, 2, reach // 2)],
        scratch_shapes=[pltpu.SemaphoreType.DMA((11,))],
        compiler_params=full,
    )(place, legendre)
    cross, listing, *first = lax.optimization_barrier((cross, wave_list, *first))
    cross = lax.ppermute(cross, "lev", [(1, 0)])
    first = [hopped(array, hop) for array, hop in zip(first, FIRST)]

    wanted = lax.all_to_all(listing.reshape(blocks, -1), "wave", 0, 0, tiled=True)

    rest = pl.pallas_call(
        rest_kernel,
        in_specs=[smem, any_space, vmem],
        out_specs=[vmem] * 8,
        out_shape=[shape_of(rows, 2, reach)] * 3 + [shape_of(3, rows, 2, reach)] * 5,
        scratch_shapes=[pltpu.SemaphoreType.DMA((8, 3))],
        compiler_params=pltpu.CompilerParams(vmem_limit_bytes=52 * 1024 * 1024),
        cost_estimate=pl.CostEstimate(flops=10**9, bytes_accessed=2**20, transcendentals=0),
    )(place, legendre, cross)
    wanted, rest = lax.optimization_barrier((wanted, rest))
    local = (wanted - block_id * slot_count).reshape(-1)
    outgoing = jnp.take(fourier, local, axis=0, mode="clip")
    outgoing, first = lax.optimization_barrier((outgoing, first))
    arrived = lax.all_to_all(outgoing, "wave", 0, 0, tiled=True)
    lone, (mine, *whole) = rest[:3], rest[3:]
    whole = [mine] + [hopped(array, hop) for array, hop in zip(whole, LAST)]
    lone = [hopped(array, hop) for array, hop in zip(lone, FIRST)]

    order = []
    for m in range(bands):
        order += [m, 15 - m, 24 + m, m, 15 - m, 16 + m]
    handled = pl.pallas_call(
        functools.partial(pick_kernel, order),
        in_specs=[vmem],
        out_specs=vmem,
        out_shape=jax.ShapeDtypeStruct((2 * bands, 3, row_count, cols), jnp.bfloat16),
        compiler_params=roomy,
    )(arrived)
    handled, whole, lone = lax.optimization_barrier((handled, whole, lone))
    fields = lax.all_to_all(handled, ("lat", "lev"), 0, 0, tiled=True)

    packed = pl.pallas_call(
        pack_kernel,
        in_specs=[vmem] * 11,
        out_specs=vmem,
        out_shape=shape_of(3, 2, bands * rows, reach),
        compiler_params=roomy,
        cost_estimate=pl.CostEstimate(
            flops=2 * 10**10, bytes_accessed=24 * 1024 * 1024, transcendentals=0
        ),
    )(*first, *lone, *whole)

    handling = lax.dynamic_index_in_dim(
        jnp.array(order, jnp.int32).reshape(2 * bands, 3), 2 * lat + lev, 0, keepdims=False
    )
    parity = jnp.take(wave_list, handling, mode="clip") % 2
    coefficients = pl.pallas_call(
        transform_kernel,
        in_specs=[smem, any_space, any_space],
        out_specs=vmem,
        out_shape=jax.ShapeDtypeStruct((2 * bands, 3, 2, width // 2, cols), jnp.bfloat16),
        scratch_shapes=[
            pltpu.VMEM((3, 2, bands * rows, 2 * cols), jnp.bfloat16),
            pltpu.VMEM((3, 2, bands * rows, reach), jnp.bfloat16),
            pltpu.VMEM((2 * bands, 3, row_count, cols), jnp.bfloat16),
            pltpu.SemaphoreType.DMA((2,)),
        ],
        compiler_params=pltpu.CompilerParams(vmem_limit_bytes=60 * 1024 * 1024),
    )(jnp.concatenate([place, parity]), packed, fields)

    owned = lax.all_to_all(coefficients, ("lat", "lev"), 0, 0, tiled=True)
    piece = width // 2
    lowest = wave_list * stride + wave_list % 2 * (stride - 1)
    lowest = jnp.broadcast_to(lowest[:, None], (slot_count, cols))
    return pl.pallas_call(
        spread_kernel,
        in_specs=[smem, vmem, vmem],
        out_specs=vmem,
        out_shape=jax.ShapeDtypeStruct((2, piece, 2, slot_count, cols), jnp.bfloat16),
        compiler_params=roomy,
    )(place, lowest, owned)


def solution(mesh):
    placed = (P("wave", "lat", "lev"), P("wave", "lat", None, "lev"), P("wave"))
    return jax.shard_map(
        shards,
        mesh=mesh,
        in_specs=placed,
        out_specs=P(None, "lat", None, "wave", "lev"),
        check_vma=False,
    )
```

```python
import functools

import jax
import jax.numpy as jnp
from jax import lax
from jax.experimental import pallas as pl
from jax.experimental.pallas import tpu as pltpu
from jax.sharding import PartitionSpec as P

NN = 2048
FIRST = (2, 6, 4)
LAST = (3, 7, 5, 1)


def band_to(lat, hop):
    if hop in (2, 3):
        return lat ^ (hop + 4 * (lat % 2))
    if hop in (6, 7):
        return lat ^ (hop - 4 * (lat % 2))
    return lat ^ hop


def band_from(lat, hop):
    if hop == 3:
        return lat ^ (7 - 4 * (lat % 2))
    if hop == 7:
        return lat ^ (3 + 4 * (lat % 2))
    return band_to(lat, hop)


def after(first, *arrays):
    return lax.optimization_barrier((first, *arrays))[1:]


def first_kernel(place, table, *refs):
    outs, cross, sems = refs[:3], *refs[3:]
    reach, cut = table.shape[3], cross.shape[3]
    copies = [
        pltpu.make_async_copy(table.at[24:28, :, :, reach - cut : reach], cross.at[0:4], sems.at[6])
    ]
    for n in range(4):
        lanes = slice(n % 2 * cut // 2, (n % 2 + 1) * cut // 2)
        copies.append(
            pltpu.make_async_copy(
                table.at[28 + n, :, :, reach - cut // 2 : reach],
                cross.at[4 + n // 2, :, :, lanes],
                sems.at[7 + n],
            )
        )
    for n, hop in enumerate(FIRST):
        band = band_to(place[0], hop)
        copies += [
            pltpu.make_async_copy(table.at[band], outs[n].at[0], sems.at[2 * n]),
            pltpu.make_async_copy(table.at[15 - band], outs[n].at[1], sems.at[2 * n + 1]),
        ]
    for copy in copies:
        copy.start()
    for copy in copies:
        copy.wait()


def rest_kernel(place, table, cross, *refs):
    outs, sems = refs[:8], refs[8]
    lat, lev = place[0], place[1]
    reach, cut = table.shape[3], cross.shape[3]
    end = cut // 2
    copies, lone = [], []
    for n, hop in enumerate((*FIRST, 0, *LAST)):
        band, out = band_to(lat, hop), outs[n]
        if n >= 3:
            copies += [
                pltpu.make_async_copy(table.at[band], out.at[0], sems.at[n, 0]),
                pltpu.make_async_copy(table.at[15 - band], out.at[1], sems.at[n, 1]),
            ]
            out = out.at[2]
        lone.append((band, out, pltpu.make_async_copy(table.at[16 + band], out, sems.at[n, 2])))
    for copy in copies:
        copy.start()

    @pl.when(lev == 0)
    def _():
        for band, out, _ in lone:
            out[:, :, 0 : reach - cut] = jnp.zeros_like(out[:, :, 0 : reach - cut])

            @pl.when(band < 4)
            def _():
                out[:, :, reach - cut :] = cross[band]

            @pl.when(band >= 4)
            def _():
                lanes = pl.ds(pl.multiple_of(band % 2 * end, end), end)
                out[:, :, reach - cut : reach - end] = jnp.zeros_like(out[:, :, 0:end])
                out[:, :, reach - end :] = cross[2 + band // 2, :, :, lanes]

    @pl.when(lev != 0)
    def _():
        for _, _, copy in lone:
            copy.start()
        for _, _, copy in lone:
            copy.wait()

    for copy in copies:
        copy.wait()


def pack_kernel(*refs):
    first, lone, whole, out = refs[:3], refs[3:6], refs[6:11], refs[11]
    rows = lone[0].shape[0]
    for n, hop in enumerate((*FIRST, 0, *LAST)):
        for f in range(3):
            if n >= 3:
                values = whole[n - 3][f]
            else:
                values = first[n][f] if f < 2 else lone[n][...]
            out[f, :, hop * rows : (hop + 1) * rows, :] = jnp.swapaxes(values, 0, 1)


def transform_kernel(place, *refs):
    packed, arrived, out, source, table, fields, sems = refs
    lat = place[0]
    rows, reach = table.shape[2] // 8, table.shape[3]
    width = reach // 4
    half = width // 2
    cols = arrived.shape[3]
    fetch = pltpu.make_async_copy(arrived, fields, sems.at[0])
    fetch.start()
    load = pltpu.make_async_copy(packed, table, sems.at[1])
    load.start()
    at_row = lax.broadcasted_iota(jnp.int32, (rows, rows), 0)
    at_col = lax.broadcasted_iota(jnp.int32, (rows, rows), 1)
    flip = (at_row + at_col == rows - 1).astype(jnp.bfloat16)
    fetch.wait()
    pairs = [(f, v) for f in range(3) for v in range(2)]
    for hop in range(8):
        band = band_from(lat, hop)
        near = [fields[2 * band + v, f, 0:rows, :] for f, v in pairs]
        far = [fields[2 * (7 - band) + v, f, rows : 2 * rows, :] for f, v in pairs]
        mirrored = jnp.dot(flip, jnp.concatenate(far, 1), preferred_element_type=jnp.float32)
        for n, (f, v) in enumerate(pairs):
            one = near[n].astype(jnp.float32)
            other = mirrored[:, n * cols : (n + 1) * cols]
            odd = place[2 + f] == 1
            other = jnp.where(odd, -other, other)
            here = (slice(hop * rows, (hop + 1) * rows), slice(v * cols, (v + 1) * cols))
            source[f, 0, *here] = (one + other).astype(jnp.bfloat16)
            source[f, 1, *here] = (one - other).astype(jnp.bfloat16)
    load.wait()
    for f in range(3):
        for p in range(2):
            for n in range(4):
                values = lax.dot_general(
                    table[f, p, :, n * width : (n + 1) * width],
                    source[f, p],
                    (((0,), (0,)), ((), ())),
                    preferred_element_type=jnp.float32,
                ).astype(jnp.bfloat16)
                for h in range(2):
                    for v in range(2):
                        out[2 * (2 * n + h) + v, f, p] = values[
                            h * half : (h + 1) * half, v * cols : (v + 1) * cols
                        ]


def pick_kernel(order, arrived, out):
    for n, slot in enumerate(order):
        out[n // 3, n % 3] = arrived[slot]


def spread_kernel(place, lowest, owned, out):
    piece, slots, cols = out.shape[1], out.shape[3], out.shape[4]
    bands = slots // 4
    up = range(bands)
    down = range(bands - 1, -1, -1)
    whole = [
        [(2 * m, 0) for m in up] + [(2 * m, 1) for m in down],
        [(2 * m + 1, 0) for m in up]
        + [(2 * m + 1, 1) for m in down]
        + [(2 * m + 1, 2) for m in up]
        + [(2 * m, 2) for m in up],
    ]
    for k in range(2):
        count = len(whole[k])
        q = lax.broadcasted_iota(jnp.int32, (piece, count, cols), 0) + (8 * k + place[0]) * piece
        held = jnp.stack([owned[n, e, 0].astype(jnp.float32) for n, e in whole[k]])
        held = jnp.transpose(held, (1, 0, 2))
        held = jnp.where(2 * q + pl.program_id(0) >= lowest[0:count][None], held, 0.0)
        out[k, :, 0, 0:count] = held.astype(jnp.bfloat16)
        if count < slots:
            out[k, :, 0, count:] = jnp.zeros((piece, slots - count, cols), jnp.bfloat16)


def shards(fourier, legendre, wave_list):
    roomy = pltpu.CompilerParams(vmem_limit_bytes=8 * 1024 * 1024)
    any_space = pl.BlockSpec(memory_space=pl.ANY)
    smem = pl.BlockSpec(memory_space=pltpu.SMEM)
    vmem = pl.BlockSpec(memory_space=pltpu.VMEM)
    lat, lev = lax.axis_index("lat"), lax.axis_index("lev")
    block_id = lax.axis_index("wave")
    slot_count, row_count, cols = fourier.shape
    bands, blocks = lax.axis_size("lat"), lax.axis_size("wave")
    rows, reach = legendre.shape[1], legendre.shape[3]
    width = reach // 4
    stride = NN // (slot_count * blocks)

    def hopped(array, hop):
        return lax.ppermute(array, "lat", [(i, band_to(i, hop)) for i in range(bands)])

    def shape_of(*dims):
        return jax.ShapeDtypeStruct(dims, jnp.bfloat16)

    place = jnp.stack([lat, lev]).astype(jnp.int32)
    full = pltpu.CompilerParams(vmem_limit_bytes=56 * 1024 * 1024)
    *first, cross = pl.pallas_call(
        first_kernel,
        in_specs=[smem, any_space],
        out_specs=[vmem] * 4,
        out_shape=[shape_of(2, rows, 2, reach)] * 3 + [shape_of(6, rows, 2, reach // 2)],
        scratch_shapes=[pltpu.SemaphoreType.DMA((11,))],
        compiler_params=full,
    )(place, legendre)
    cross, listing, *first = lax.optimization_barrier((cross, wave_list, *first))
    cross = lax.ppermute(cross, "lev", [(1, 0)])
    first = [hopped(array, hop) for array, hop in zip(first, FIRST)]

    wanted = lax.all_to_all(listing.reshape(blocks, -1), "wave", 0, 0, tiled=True)

    rest = pl.pallas_call(
        rest_kernel,
        in_specs=[smem, any_space, vmem],
        out_specs=[vmem] * 8,
        out_shape=[shape_of(rows, 2, reach)] * 3 + [shape_of(3, rows, 2, reach)] * 5,
        scratch_shapes=[pltpu.SemaphoreType.DMA((8, 3))],
        compiler_params=pltpu.CompilerParams(vmem_limit_bytes=48 * 1024 * 1024),
        cost_estimate=pl.CostEstimate(flops=10**9, bytes_accessed=2**20, transcendentals=0),
    )(place, legendre, cross)
    wanted, rest = lax.optimization_barrier((wanted, rest))
    local = (wanted - block_id * slot_count).reshape(-1)
    outgoing = jnp.take(fourier, local, axis=0, mode="clip")
    outgoing, first = lax.optimization_barrier((outgoing, first))
    arrived = lax.all_to_all(outgoing, "wave", 0, 0, tiled=True)
    lone, (mine, *whole) = rest[:3], rest[3:]
    whole = [mine] + [hopped(array, hop) for array, hop in zip(whole, LAST)]
    lone = [hopped(array, hop) for array, hop in zip(lone, FIRST)]

    order = []
    for m in range(bands):
        order += [m, 15 - m, 24 + m, m, 15 - m, 16 + m]
    handled = pl.pallas_call(
        functools.partial(pick_kernel, order),
        in_specs=[vmem],
        out_specs=vmem,
        out_shape=jax.ShapeDtypeStruct((2 * bands, 3, row_count, cols), jnp.bfloat16),
        compiler_params=roomy,
    )(arrived)
    handled, whole, lone = lax.optimization_barrier((handled, whole, lone))
    fields = lax.all_to_all(handled, ("lat", "lev"), 0, 0, tiled=True)

    packed = pl.pallas_call(
        pack_kernel,
        in_specs=[vmem] * 11,
        out_specs=vmem,
        out_shape=shape_of(3, 2, bands * rows, reach),
        compiler_params=roomy,
        cost_estimate=pl.CostEstimate(
            flops=2 * 10**10, bytes_accessed=24 * 1024 * 1024, transcendentals=0
        ),
    )(*first, *lone, *whole)

    handling = lax.dynamic_index_in_dim(
        jnp.array(order, jnp.int32).reshape(2 * bands, 3), 2 * lat + lev, 0, keepdims=False
    )
    parity = jnp.take(wave_list, handling, mode="clip") % 2
    coefficients = pl.pallas_call(
        transform_kernel,
        in_specs=[smem, any_space, any_space],
        out_specs=vmem,
        out_shape=jax.ShapeDtypeStruct((2 * bands, 3, 2, width // 2, cols), jnp.bfloat16),
        scratch_shapes=[
            pltpu.VMEM((3, 2, bands * rows, 2 * cols), jnp.bfloat16),
            pltpu.VMEM((3, 2, bands * rows, reach), jnp.bfloat16),
            pltpu.VMEM((2 * bands, 3, row_count, cols), jnp.bfloat16),
            pltpu.SemaphoreType.DMA((2,)),
        ],
        compiler_params=pltpu.CompilerParams(vmem_limit_bytes=60 * 1024 * 1024),
    )(jnp.concatenate([place, parity]), packed, fields)

    owned = lax.all_to_all(coefficients, ("lat", "lev"), 0, 0, tiled=True)
    piece = width // 2
    lowest = wave_list * stride + wave_list % 2 * (stride - 1)
    lowest = jnp.broadcast_to(lowest[:, None], (slot_count, cols))
    return pl.pallas_call(
        spread_kernel,
        grid=(2,),
        in_specs=[
            smem,
            pl.BlockSpec((slot_count, cols), lambda p: (0, 0)),
            pl.BlockSpec((2 * bands, 3, 1, piece, cols), lambda p: (0, 0, p, 0, 0)),
        ],
        out_specs=pl.BlockSpec((2, piece, 1, slot_count, cols), lambda p: (0, 0, p, 0, 0)),
        out_shape=jax.ShapeDtypeStruct((2, piece, 2, slot_count, cols), jnp.bfloat16),
        compiler_params=roomy,
    )(place, lowest, owned)


def solution(mesh):
    placed = (P("wave", "lat", "lev"), P("wave", "lat", None, "lev"), P("wave"))
    return jax.shard_map(
        shards,
        mesh=mesh,
        in_specs=placed,
        out_specs=P(None, "lat", None, "wave", "lev"),
        check_vma=False,
    )
```

```python
import functools

import jax
import jax.numpy as jnp
from jax import lax
from jax.experimental import pallas as pl
from jax.experimental.pallas import tpu as pltpu
from jax.sharding import PartitionSpec as P

NN = 2048
FIRST = (4, 2, 6)
LAST = (5, 3, 7, 1)


def band_to(lat, hop):
    if hop in (2, 3):
        return lat ^ (hop + 4 * (lat % 2))
    if hop in (6, 7):
        return lat ^ (hop - 4 * (lat % 2))
    return lat ^ hop


def band_from(lat, hop):
    if hop == 3:
        return lat ^ (7 - 4 * (lat % 2))
    if hop == 7:
        return lat ^ (3 + 4 * (lat % 2))
    return band_to(lat, hop)


def after(first, *arrays):
    return lax.optimization_barrier((first, *arrays))[1:]


def first_kernel(place, table, *refs):
    outs, cross, sems = refs[:3], *refs[3:]
    reach, cut = table.shape[3], cross.shape[3]
    copies = [
        pltpu.make_async_copy(table.at[24:28, :, :, reach - cut : reach], cross.at[0:4], sems.at[6])
    ]
    for n in range(4):
        lanes = slice(n % 2 * cut // 2, (n % 2 + 1) * cut // 2)
        copies.append(
            pltpu.make_async_copy(
                table.at[28 + n, :, :, reach - cut // 2 : reach],
                cross.at[4 + n // 2, :, :, lanes],
                sems.at[7 + n],
            )
        )
    for n, hop in enumerate(FIRST):
        band = band_to(place[0], hop)
        copies += [
            pltpu.make_async_copy(table.at[band], outs[n].at[0], sems.at[2 * n]),
            pltpu.make_async_copy(table.at[15 - band], outs[n].at[1], sems.at[2 * n + 1]),
        ]
    for copy in copies:
        copy.start()
    for copy in copies:
        copy.wait()


def rest_kernel(place, table, cross, *refs):
    outs, sems = refs[:8], refs[8]
    lat, lev = place[0], place[1]
    reach, cut = table.shape[3], cross.shape[3]
    end = cut // 2
    copies, lone = [], []
    for n, hop in enumerate((*FIRST, 0, *LAST)):
        band, out = band_to(lat, hop), outs[n]
        if n >= 3:
            copies += [
                pltpu.make_async_copy(table.at[band], out.at[0], sems.at[n, 0]),
                pltpu.make_async_copy(table.at[15 - band], out.at[1], sems.at[n, 1]),
            ]
            out = out.at[2]
        lone.append((band, out, pltpu.make_async_copy(table.at[16 + band], out, sems.at[n, 2])))
    for copy in copies:
        copy.start()

    @pl.when(lev == 0)
    def _():
        for band, out, _ in lone:
            out[:, :, 0 : reach - cut] = jnp.zeros_like(out[:, :, 0 : reach - cut])

            @pl.when(band < 4)
            def _():
                out[:, :, reach - cut :] = cross[band]

            @pl.when(band >= 4)
            def _():
                lanes = pl.ds(pl.multiple_of(band % 2 * end, end), end)
                out[:, :, reach - cut : reach - end] = jnp.zeros_like(out[:, :, 0:end])
                out[:, :, reach - end :] = cross[2 + band // 2, :, :, lanes]

    @pl.when(lev != 0)
    def _():
        for _, _, copy in lone:
            copy.start()
        for _, _, copy in lone:
            copy.wait()

    for copy in copies:
        copy.wait()


def pack_kernel(*refs):
    first, lone, whole, out = refs[:3], refs[3:6], refs[6:11], refs[11]
    rows = lone[0].shape[0]
    for n, hop in enumerate((*FIRST, 0, *LAST)):
        for f in range(3):
            if n >= 3:
                values = whole[n - 3][f]
            else:
                values = first[n][f] if f < 2 else lone[n][...]
            out[f, :, hop * rows : (hop + 1) * rows, :] = jnp.swapaxes(values, 0, 1)


def transform_kernel(place, table, fields, out, source):
    lat = place[0]
    rows, reach = table.shape[2] // 8, table.shape[3]
    width = reach // 4
    half = width // 2
    cols = fields.shape[3]
    odd = place[2 + pl.program_id(0)] == 1
    at_row = lax.broadcasted_iota(jnp.int32, (rows, rows), 0)
    at_col = lax.broadcasted_iota(jnp.int32, (rows, rows), 1)
    flip = (at_row + at_col == rows - 1).astype(jnp.bfloat16)
    for hop in range(8):
        band = band_from(lat, hop)
        here = slice(hop * rows, (hop + 1) * rows)
        near = [fields[2 * band + v, 0, 0:rows, :] for v in range(2)]
        far = [fields[2 * (7 - band) + v, 0, rows : 2 * rows, :] for v in range(2)]
        one = jnp.concatenate(near, 1).astype(jnp.float32)
        other = jnp.dot(flip, jnp.concatenate(far, 1), preferred_element_type=jnp.float32)
        other = jnp.where(odd, -other, other)
        source[0, here, :] = (one + other).astype(jnp.bfloat16)
        source[1, here, :] = (one - other).astype(jnp.bfloat16)
    for p in range(2):
        for n in range(4):
            values = lax.dot_general(
                table[0, p, :, n * width : (n + 1) * width],
                source[p],
                (((0,), (0,)), ((), ())),
                preferred_element_type=jnp.float32,
            ).astype(jnp.bfloat16)
            for h in range(2):
                for v in range(2):
                    out[2 * (2 * n + h) + v, 0, p] = values[
                        h * half : (h + 1) * half, v * cols : (v + 1) * cols
                    ]


def pick_kernel(order, arrived, out):
    part = len(order) // 4
    for quarter in range(4):

        @pl.when(pl.program_id(0) == quarter)
        def _():
            for n in range(part):
                out[n // 3, n % 3] = arrived[order[quarter * part + n]]


def spread_kernel(place, lowest, owned, out):
    piece, slots, cols = out.shape[1], out.shape[3], out.shape[4]
    bands = slots // 4
    up = range(bands)
    down = range(bands - 1, -1, -1)
    whole = [
        [(2 * m, 0) for m in up] + [(2 * m, 1) for m in down],
        [(2 * m + 1, 0) for m in up]
        + [(2 * m + 1, 1) for m in down]
        + [(2 * m + 1, 2) for m in up]
        + [(2 * m, 2) for m in up],
    ]
    for k in range(2):
        count = len(whole[k])
        q = lax.broadcasted_iota(jnp.int32, (piece, count, cols), 0) + (8 * k + place[0]) * piece
        held = jnp.stack([owned[n, e, 0].astype(jnp.float32) for n, e in whole[k]])
        held = jnp.transpose(held, (1, 0, 2))
        held = jnp.where(2 * q + pl.program_id(0) >= lowest[0:count][None], held, 0.0)
        out[k, :, 0, 0:count] = held.astype(jnp.bfloat16)
        if count < slots:
            out[k, :, 0, count:] = jnp.zeros((piece, slots - count, cols), jnp.bfloat16)


def shards(fourier, legendre, wave_list):
    roomy = pltpu.CompilerParams(vmem_limit_bytes=8 * 1024 * 1024)
    any_space = pl.BlockSpec(memory_space=pl.ANY)
    smem = pl.BlockSpec(memory_space=pltpu.SMEM)
    vmem = pl.BlockSpec(memory_space=pltpu.VMEM)
    lat, lev = lax.axis_index("lat"), lax.axis_index("lev")
    block_id = lax.axis_index("wave")
    slot_count, row_count, cols = fourier.shape
    bands, blocks = lax.axis_size("lat"), lax.axis_size("wave")
    rows, reach = legendre.shape[1], legendre.shape[3]
    width = reach // 4
    stride = NN // (slot_count * blocks)

    def hopped(array, hop):
        return lax.ppermute(array, "lat", [(i, band_to(i, hop)) for i in range(bands)])

    def shape_of(*dims):
        return jax.ShapeDtypeStruct(dims, jnp.bfloat16)

    place = jnp.stack([lat, lev]).astype(jnp.int32)
    full = pltpu.CompilerParams(vmem_limit_bytes=56 * 1024 * 1024)
    *first, cross = pl.pallas_call(
        first_kernel,
        in_specs=[smem, any_space],
        out_specs=[vmem] * 4,
        out_shape=[shape_of(2, rows, 2, reach)] * 3 + [shape_of(6, rows, 2, reach // 2)],
        scratch_shapes=[pltpu.SemaphoreType.DMA((11,))],
        compiler_params=full,
    )(place, legendre)
    cross, listing, *first = lax.optimization_barrier((cross, wave_list, *first))
    cross = lax.ppermute(cross, "lev", [(1, 0)])
    first = [hopped(array, hop) for array, hop in zip(first, FIRST)]

    wanted = lax.all_to_all(listing.reshape(blocks, -1), "wave", 0, 0, tiled=True)

    rest = pl.pallas_call(
        rest_kernel,
        in_specs=[smem, any_space, vmem],
        out_specs=[vmem] * 8,
        out_shape=[shape_of(rows, 2, reach)] * 3 + [shape_of(3, rows, 2, reach)] * 5,
        scratch_shapes=[pltpu.SemaphoreType.DMA((8, 3))],
        compiler_params=pltpu.CompilerParams(vmem_limit_bytes=48 * 1024 * 1024),
        cost_estimate=pl.CostEstimate(flops=10**9, bytes_accessed=2**20, transcendentals=0),
    )(place, legendre, cross)
    wanted, rest = lax.optimization_barrier((wanted, rest))
    local = (wanted - block_id * slot_count).reshape(-1)
    outgoing = jnp.take(fourier, local, axis=0, mode="clip")
    outgoing, first = lax.optimization_barrier((outgoing, first))
    arrived = lax.all_to_all(outgoing, "wave", 0, 0, tiled=True)
    lone, (mine, *whole) = rest[:3], rest[3:]
    whole = [mine] + [hopped(array, hop) for array, hop in zip(whole, LAST)]
    lone = [hopped(array, hop) for array, hop in zip(lone, FIRST)]

    order = []
    for m in range(bands):
        order += [m, 15 - m, 24 + m, m, 15 - m, 16 + m]
    handled = pl.pallas_call(
        functools.partial(pick_kernel, order),
        grid=(4,),
        in_specs=[pl.BlockSpec((slot_count, row_count, cols), lambda n: (0, 0, 0))],
        out_specs=pl.BlockSpec((bands // 2, 3, row_count, cols), lambda n: (n, 0, 0, 0)),
        out_shape=shape_of(2 * bands, 3, row_count, cols),
        compiler_params=pltpu.CompilerParams(vmem_limit_bytes=60 * 1024 * 1024),
    )(arrived)
    handled, whole, lone = lax.optimization_barrier((handled, whole, lone))
    fields = lax.all_to_all(handled, ("lat", "lev"), 0, 0, tiled=True)

    packed = pl.pallas_call(
        pack_kernel,
        in_specs=[vmem] * 11,
        out_specs=vmem,
        out_shape=shape_of(3, 2, bands * rows, reach),
        compiler_params=roomy,
        cost_estimate=pl.CostEstimate(
            flops=2 * 10**10, bytes_accessed=24 * 1024 * 1024, transcendentals=0
        ),
    )(*first, *lone, *whole)

    handling = lax.dynamic_index_in_dim(
        jnp.array(order, jnp.int32).reshape(2 * bands, 3), 2 * lat + lev, 0, keepdims=False
    )
    parity = jnp.take(wave_list, handling, mode="clip") % 2
    coefficients = pl.pallas_call(
        transform_kernel,
        grid=(3,),
        in_specs=[
            smem,
            pl.BlockSpec((1, 2, bands * rows, reach), lambda f: (f, 0, 0, 0)),
            pl.BlockSpec((2 * bands, 1, row_count, cols), lambda f: (0, f, 0, 0)),
        ],
        out_specs=pl.BlockSpec((2 * bands, 1, 2, width // 2, cols), lambda f: (0, f, 0, 0, 0)),
        out_shape=shape_of(2 * bands, 3, 2, width // 2, cols),
        scratch_shapes=[pltpu.VMEM((2, bands * rows, 2 * cols), jnp.bfloat16)],
        compiler_params=pltpu.CompilerParams(vmem_limit_bytes=60 * 1024 * 1024),
    )(jnp.concatenate([place, parity]), packed, fields)

    owned = lax.all_to_all(coefficients, ("lat", "lev"), 0, 0, tiled=True)
    piece = width // 2
    lowest = wave_list * stride + wave_list % 2 * (stride - 1)
    lowest = jnp.broadcast_to(lowest[:, None], (slot_count, cols))
    return pl.pallas_call(
        spread_kernel,
        grid=(2,),
        in_specs=[
            smem,
            pl.BlockSpec((slot_count, cols), lambda p: (0, 0)),
            pl.BlockSpec((2 * bands, 3, 1, piece, cols), lambda p: (0, 0, p, 0, 0)),
        ],
        out_specs=pl.BlockSpec((2, piece, 1, slot_count, cols), lambda p: (0, 0, p, 0, 0)),
        out_shape=jax.ShapeDtypeStruct((2, piece, 2, slot_count, cols), jnp.bfloat16),
        compiler_params=roomy,
    )(place, lowest, owned)


def solution(mesh):
    placed = (P("wave", "lat", "lev"), P("wave", "lat", None, "lev"), P("wave"))
    return jax.shard_map(
        shards,
        mesh=mesh,
        in_specs=placed,
        out_specs=P(None, "lat", None, "wave", "lev"),
        check_vma=False,
    )
```

```python
import functools

import jax
import jax.numpy as jnp
from jax import lax
from jax.experimental import pallas as pl
from jax.experimental.pallas import tpu as pltpu
from jax.sharding import PartitionSpec as P

NN = 2048
FIRST = (4, 2, 6)
LAST = (5, 3, 7, 1)


def band_to(lat, hop):
    if hop in (2, 3):
        return lat ^ (hop + 4 * (lat % 2))
    if hop in (6, 7):
        return lat ^ (hop - 4 * (lat % 2))
    return lat ^ hop


def band_from(lat, hop):
    if hop == 3:
        return lat ^ (7 - 4 * (lat % 2))
    if hop == 7:
        return lat ^ (3 + 4 * (lat % 2))
    return band_to(lat, hop)


def after(first, *arrays):
    return lax.optimization_barrier((first, *arrays))[1:]


def first_kernel(place, table, *refs):
    outs, cross, sems = refs[:3], *refs[3:]
    reach, cut = table.shape[3], cross.shape[3]
    copies = [
        pltpu.make_async_copy(table.at[24:28, :, :, reach - cut : reach], cross.at[0:4], sems.at[6])
    ]
    for n in range(4):
        lanes = slice(n % 2 * cut // 2, (n % 2 + 1) * cut // 2)
        copies.append(
            pltpu.make_async_copy(
                table.at[28 + n, :, :, reach - cut // 2 : reach],
                cross.at[4 + n // 2, :, :, lanes],
                sems.at[7 + n],
            )
        )
    for n, hop in enumerate(FIRST):
        band = band_to(place[0], hop)
        copies += [
            pltpu.make_async_copy(table.at[band], outs[n].at[0], sems.at[2 * n]),
            pltpu.make_async_copy(table.at[15 - band], outs[n].at[1], sems.at[2 * n + 1]),
        ]
    for copy in copies:
        copy.start()
    for copy in copies:
        copy.wait()


def rest_kernel(place, table, cross, *refs):
    outs, sems = refs[:8], refs[8]
    lat, lev = place[0], place[1]
    reach, cut = table.shape[3], cross.shape[3]
    end = cut // 2
    copies, lone = [], []
    for n, hop in enumerate((*FIRST, 0, *LAST)):
        band, out = band_to(lat, hop), outs[n]
        if n >= 3:
            copies += [
                pltpu.make_async_copy(table.at[band], out.at[0], sems.at[n, 0]),
                pltpu.make_async_copy(table.at[15 - band], out.at[1], sems.at[n, 1]),
            ]
            out = out.at[2]
        lone.append((band, out, pltpu.make_async_copy(table.at[16 + band], out, sems.at[n, 2])))
    for copy in copies:
        copy.start()

    @pl.when(lev == 0)
    def _():
        for band, out, _ in lone:
            out[:, :, 0 : reach - cut] = jnp.zeros_like(out[:, :, 0 : reach - cut])

            @pl.when(band < 4)
            def _():
                out[:, :, reach - cut :] = cross[band]

            @pl.when(band >= 4)
            def _():
                lanes = pl.ds(pl.multiple_of(band % 2 * end, end), end)
                out[:, :, reach - cut : reach - end] = jnp.zeros_like(out[:, :, 0:end])
                out[:, :, reach - end :] = cross[2 + band // 2, :, :, lanes]

    @pl.when(lev != 0)
    def _():
        for _, _, copy in lone:
            copy.start()
        for _, _, copy in lone:
            copy.wait()

    for copy in copies:
        copy.wait()


def pack_kernel(*refs):
    first, lone, whole, out = refs[:3], refs[3:6], refs[6:11], refs[11]
    rows = lone[0].shape[0]
    for n, hop in enumerate((*FIRST, 0, *LAST)):
        for f in range(3):
            if n >= 3:
                values = whole[n - 3][f]
            else:
                values = first[n][f] if f < 2 else lone[n][...]
            out[f, :, hop * rows : (hop + 1) * rows, :] = jnp.swapaxes(values, 0, 1)


def transform_kernel(place, table, fields, out, source):
    lat = place[0]
    rows, reach = table.shape[2] // 8, table.shape[3]
    width = reach // 4
    half = width // 2
    cols = fields.shape[3]
    odd = place[2 + pl.program_id(0)] == 1
    at_row = lax.broadcasted_iota(jnp.int32, (rows, rows), 0)
    at_col = lax.broadcasted_iota(jnp.int32, (rows, rows), 1)
    flip = (at_row + at_col == rows - 1).astype(jnp.bfloat16)
    for hop in range(8):
        band = band_from(lat, hop)
        here = slice(hop * rows, (hop + 1) * rows)
        near = [fields[2 * band + v, 0, 0:rows, :] for v in range(2)]
        far = [fields[2 * (7 - band) + v, 0, rows : 2 * rows, :] for v in range(2)]
        one = jnp.concatenate(near, 1).astype(jnp.float32)
        other = jnp.dot(flip, jnp.concatenate(far, 1), preferred_element_type=jnp.float32)
        other = jnp.where(odd, -other, other)
        source[0, here, :] = (one + other).astype(jnp.bfloat16)
        source[1, here, :] = (one - other).astype(jnp.bfloat16)
    for p in range(2):
        for n in range(4):
            values = lax.dot_general(
                table[0, p, :, n * width : (n + 1) * width],
                source[p],
                (((0,), (0,)), ((), ())),
                preferred_element_type=jnp.float32,
            ).astype(jnp.bfloat16)
            for h in range(2):
                for v in range(2):
                    out[2 * (2 * n + h) + v, 0, p] = values[
                        h * half : (h + 1) * half, v * cols : (v + 1) * cols
                    ]


def pick_kernel(order, arrived, out):
    part = len(order) // 4
    for quarter in range(4):

        @pl.when(pl.program_id(0) == quarter)
        def _():
            for n in range(part):
                out[n // 3, n % 3] = arrived[order[quarter * part + n]]


def spread_kernel(place, lowest, owned, out):
    piece, slots, cols = out.shape[1], out.shape[3], out.shape[4]
    bands = slots // 4
    up = range(bands)
    down = range(bands - 1, -1, -1)
    whole = [
        [(2 * m, 0) for m in up] + [(2 * m, 1) for m in down],
        [(2 * m + 1, 0) for m in up]
        + [(2 * m + 1, 1) for m in down]
        + [(2 * m + 1, 2) for m in up]
        + [(2 * m, 2) for m in up],
    ]
    for k in range(2):
        count = len(whole[k])
        q = lax.broadcasted_iota(jnp.int32, (piece, count, cols), 0) + (8 * k + place[0]) * piece
        held = jnp.stack([owned[n, e, 0].astype(jnp.float32) for n, e in whole[k]])
        held = jnp.transpose(held, (1, 0, 2))
        held = jnp.where(2 * q + pl.program_id(0) >= lowest[0:count][None], held, 0.0)
        out[k, :, 0, 0:count] = held.astype(jnp.bfloat16)
        if count < slots:
            out[k, :, 0, count:] = jnp.zeros((piece, slots - count, cols), jnp.bfloat16)


def shards(fourier, legendre, wave_list):
    roomy = pltpu.CompilerParams(vmem_limit_bytes=8 * 1024 * 1024)
    any_space = pl.BlockSpec(memory_space=pl.ANY)
    smem = pl.BlockSpec(memory_space=pltpu.SMEM)
    vmem = pl.BlockSpec(memory_space=pltpu.VMEM)
    lat, lev = lax.axis_index("lat"), lax.axis_index("lev")
    block_id = lax.axis_index("wave")
    slot_count, row_count, cols = fourier.shape
    bands, blocks = lax.axis_size("lat"), lax.axis_size("wave")
    rows, reach = legendre.shape[1], legendre.shape[3]
    width = reach // 4
    stride = NN // (slot_count * blocks)

    def hopped(array, hop):
        return lax.ppermute(array, "lat", [(i, band_to(i, hop)) for i in range(bands)])

    def shape_of(*dims):
        return jax.ShapeDtypeStruct(dims, jnp.bfloat16)

    place = jnp.stack([lat, lev]).astype(jnp.int32)
    full = pltpu.CompilerParams(vmem_limit_bytes=56 * 1024 * 1024)
    *first, cross = pl.pallas_call(
        first_kernel,
        in_specs=[smem, any_space],
        out_specs=[vmem] * 4,
        out_shape=[shape_of(2, rows, 2, reach)] * 3 + [shape_of(6, rows, 2, reach // 2)],
        scratch_shapes=[pltpu.SemaphoreType.DMA((11,))],
        compiler_params=full,
    )(place, legendre)
    cross, listing, *first = lax.optimization_barrier((cross, wave_list, *first))
    cross = lax.ppermute(cross, "lev", [(1, 0)])
    first = [hopped(array, hop) for array, hop in zip(first, FIRST)]

    wanted = lax.all_to_all(listing.reshape(blocks, -1), "wave", 0, 0, tiled=True)

    local = (wanted - block_id * slot_count).reshape(-1)
    outgoing = jnp.take(fourier, local, axis=0, mode="clip")
    outgoing, cross, first[:2] = lax.optimization_barrier((outgoing, cross, first[:2]))
    arrived = lax.all_to_all(outgoing, "wave", 0, 0, tiled=True)
    rest = pl.pallas_call(
        rest_kernel,
        in_specs=[smem, any_space, vmem],
        out_specs=[vmem] * 8,
        out_shape=[shape_of(rows, 2, reach)] * 3 + [shape_of(3, rows, 2, reach)] * 5,
        scratch_shapes=[pltpu.SemaphoreType.DMA((8, 3))],
        compiler_params=pltpu.CompilerParams(vmem_limit_bytes=48 * 1024 * 1024),
        cost_estimate=pl.CostEstimate(flops=10**9, bytes_accessed=2**20, transcendentals=0),
    )(place, legendre, cross)
    lone, (mine, *whole) = rest[:3], rest[3:]
    whole = [mine] + [hopped(array, hop) for array, hop in zip(whole, LAST)]
    lone = [hopped(array, hop) for array, hop in zip(lone, FIRST)]

    order = []
    for m in range(bands):
        order += [m, 15 - m, 24 + m, m, 15 - m, 16 + m]
    handled = pl.pallas_call(
        functools.partial(pick_kernel, order),
        grid=(4,),
        in_specs=[pl.BlockSpec((slot_count, row_count, cols), lambda n: (0, 0, 0))],
        out_specs=pl.BlockSpec((bands // 2, 3, row_count, cols), lambda n: (n, 0, 0, 0)),
        out_shape=shape_of(2 * bands, 3, row_count, cols),
        compiler_params=pltpu.CompilerParams(vmem_limit_bytes=60 * 1024 * 1024),
    )(arrived)
    handled, first, whole, lone = lax.optimization_barrier((handled, first, whole, lone))
    fields = lax.all_to_all(handled, ("lat", "lev"), 0, 0, tiled=True)

    packed = pl.pallas_call(
        pack_kernel,
        in_specs=[vmem] * 11,
        out_specs=vmem,
        out_shape=shape_of(3, 2, bands * rows, reach),
        compiler_params=roomy,
        cost_estimate=pl.CostEstimate(
            flops=2 * 10**10, bytes_accessed=24 * 1024 * 1024, transcendentals=0
        ),
    )(*first, *lone, *whole)

    handling = lax.dynamic_index_in_dim(
        jnp.array(order, jnp.int32).reshape(2 * bands, 3), 2 * lat + lev, 0, keepdims=False
    )
    parity = jnp.take(wave_list, handling, mode="clip") % 2
    coefficients = pl.pallas_call(
        transform_kernel,
        grid=(3,),
        in_specs=[
            smem,
            pl.BlockSpec((1, 2, bands * rows, reach), lambda f: (f, 0, 0, 0)),
            pl.BlockSpec((2 * bands, 1, row_count, cols), lambda f: (0, f, 0, 0)),
        ],
        out_specs=pl.BlockSpec((2 * bands, 1, 2, width // 2, cols), lambda f: (0, f, 0, 0, 0)),
        out_shape=shape_of(2 * bands, 3, 2, width // 2, cols),
        scratch_shapes=[pltpu.VMEM((2, bands * rows, 2 * cols), jnp.bfloat16)],
        compiler_params=pltpu.CompilerParams(vmem_limit_bytes=60 * 1024 * 1024),
    )(jnp.concatenate([place, parity]), packed, fields)

    owned = lax.all_to_all(coefficients, ("lat", "lev"), 0, 0, tiled=True)
    piece = width // 2
    lowest = wave_list * stride + wave_list % 2 * (stride - 1)
    lowest = jnp.broadcast_to(lowest[:, None], (slot_count, cols))
    return pl.pallas_call(
        spread_kernel,
        grid=(2,),
        in_specs=[
            smem,
            pl.BlockSpec((slot_count, cols), lambda p: (0, 0)),
            pl.BlockSpec((2 * bands, 3, 1, piece, cols), lambda p: (0, 0, p, 0, 0)),
        ],
        out_specs=pl.BlockSpec((2, piece, 1, slot_count, cols), lambda p: (0, 0, p, 0, 0)),
        out_shape=jax.ShapeDtypeStruct((2, piece, 2, slot_count, cols), jnp.bfloat16),
        compiler_params=roomy,
    )(place, lowest, owned)


def solution(mesh):
    placed = (P("wave", "lat", "lev"), P("wave", "lat", None, "lev"), P("wave"))
    return jax.shard_map(
        shards,
        mesh=mesh,
        in_specs=placed,
        out_specs=P(None, "lat", None, "wave", "lev"),
        check_vma=False,
    )
```
